32 devices in a mesh: feat: 4 (over y, x), dp: 8 (over z, core).
Axes of the slice: x: 2, y: 2, z: 4, core: 2. Of those that a mesh axis runs over, the one named last changes fastest.
Arguments:
- text_rows: bfloat16 [1024, 8192], P('dp', 'feat'), may hold values from -6 to 6
- q_weight: bfloat16 [8192, 8192], P(None, 'feat'), may hold values from -0.0625 to 0.0625
- features: bfloat16 [8, 1024, 7680], P('dp', None, 'feat'), may hold values from -6 to 6
- kv_weight: bfloat16 [7680, 2048], P('feat'), may hold values from -0.0625 to 0.0625
- q_gain: float32 [128], replicated, may hold values from 0.7 to 2.6
- k_gain: float32 [128], replicated, may hold values from 0.7 to 2.6
- attn_gate: float32 [1], replicated, may hold values from 0.5 to 2
- image_ids: int32 [128, 2], P('dp'), may hold values from 0 to 7, all different within a row; in each aligned block of 16 rows (0 to 15, 16 to 31, ...) at most 8 rows name the same one
- image_slot: int32 [8], replicated, may hold values from 0 to 7, each once
Outputs:
- attended: bfloat16 [1024, 8192], P('dp', 'feat')
The draws below stay inside these ranges and needn't reach their ends.
Inputs may be any that keep to these rules, and one draw needn't show every extreme that they name: `image_ids`: each request names two different images; among the requests of one index of dp (aligned blocks of 16 requests) no image is named more than 8 times, a bound that some block reaches. Each position once; image i lies at position image_slot[i].
All inputs are finite; a program needn't handle non-finite values.
Results may differ from the reference program's by a relative error of at most 0.009.
The reference program's roundings to bfloat16 on the way count: a program that leaves them out, or rounds other values in their place, can miss the bound.
Values may be sent and summed in bfloat16 or wider, within the bound.
A program may use at most 128 MiB of HBM per device.

```python
import math
import jax
import jax.numpy as jnp
import numpy as np
from jax import lax

D = 8192
HEADS = 64
KVH = 8
HD = 128
FEAT = 7680
TEXT = 8
RQ_DEV = 16
VT = 1024
NIMG = 8
REQUESTS = 128
ROWS = 1024
CAP = 8


def block_scale(key, dims, split, least, top_value):
    loudness, own = 1.0, jax.random.fold_in(key, 6)
    for axis_at, shards_of in split:
        draws = jnp.exp(jax.random.uniform(jax.random.fold_in(own, axis_at), (shards_of,), jnp.float32, least / len(split), top_value / len(split)))
        loudness = loudness * jnp.repeat(draws, dims[axis_at] // shards_of).reshape([-1 if axis == axis_at else 1 for axis in range(len(dims))])
    return loudness


def deal_out(stream_key, own, number, rows, count, top, limit, lean):
    ranking = jax.random.permutation(stream_key, count)
    packed, common = load_shares(count, rows * top, limit, lean, True), load_shares(count, rows * top, limit, lean, False)
    places = jnp.arange(count)

    def named(sizes, offset_by):
        used = int((sizes > 0).sum())
        fixed = max(1, used // 4)
        passed = fixed + (places - fixed + offset_by * (used - fixed)) % max(1, count - fixed)
        return jnp.zeros((count,), jnp.int32).at[ranking[jnp.where(places < fixed, places, passed)]].set(jnp.asarray(sizes, jnp.int32))

    sizes = jnp.where(number % 4 == 0, named(packed, number // 4), named(common, number - number // 4 - 1))
    mixed = jax.random.permutation(jax.random.fold_in(own, 3), count)
    source_of, sink = mixed[0:count // 2 * 2:2], mixed[1:count // 2 * 2:2]
    slack = jnp.minimum(sizes[source_of] - 1, limit - sizes[sink]) // 2
    slack = jnp.where((source_of == ranking[0]) | (sink == ranking[0]) | (sizes[sink] == 0), 0, jnp.maximum(slack, 0))
    passed = jax.random.randint(jax.random.fold_in(own, 4), (count // 2,), 0, 1 << 20) % (slack + 1)
    sizes = sizes.at[source_of].add(-passed).at[sink].add(passed)
    members = jnp.searchsorted(jnp.cumsum(sizes), jnp.arange(rows * top), side="right").astype(jnp.int32)
    table = members.reshape(top, rows).T
    table = table[jax.random.permutation(jax.random.fold_in(own, 1), rows)]
    offset_by = jax.random.randint(jax.random.fold_in(own, 2), (rows, 1), 0, top)
    return jnp.take_along_axis(table, (jnp.arange(top)[None, :] + offset_by) % top, axis=1)


def load_shares(amount, total, most, skew, full):
    weights = [(1 << 20) // math.isqrt(rank ** skew) + 1 for rank in range(1, amount + 1)]
    largest = most if full else min(most, max(-(-total // amount), total * weights[0] // sum(weights)))
    least = 1 if total - largest >= amount - 1 else 0
    given, spare = [largest] + [least] * (amount - 1), total - largest - least * (amount - 1)
    while spare > 0:
        free = [i for i in range(1, amount) if given[i] < largest] or [i for i in range(1, amount) if given[i] < most]
        whole, left = sum([weights[i] for i in free]), spare
        for i in free:
            more = min(most - given[i], max(1, left * weights[i] // whole), spare)
            given[i] = given[i] + more
            spare = spare - more
    return np.array(given)


def scatter_about(own_key, dims, scale, bound, split=(), kind=jnp.bfloat16):
    values = jax.random.normal(own_key, dims, jnp.float32) * scale
    if len(split) > 0:
        values = block_scale(own_key, dims, split, -0.22, 0.18) * values
    return jnp.clip(values, min=-bound, max=bound).astype(kind)


def setup_inputs(seed: int = 0) -> dict:
    splits = jax.random.split(jax.random.key(seed), 10)
    text_rows = scatter_about(splits[0], (ROWS, D), 1.0, 6.0, ((0, 8), (1, 4)))
    q_weight = scatter_about(splits[1], (D, HEADS * HD), D ** -0.5, 0.0625, ((1, 4),))
    features = scatter_about(splits[2], (NIMG, VT, FEAT), 1.0, 6.0, ((0, 8), (2, 4)))
    kv_weight = scatter_about(splits[3], (FEAT, KVH * 2 * HD), FEAT ** -0.5, 0.0625, ((0, 4),))
    q_gain = jnp.clip(jnp.exp(jax.random.uniform(splits[4], (HD,), jnp.float32, math.log(0.7), math.log(2.6))), 0.7, 2.6)
    k_gain = jnp.clip(jnp.exp(jax.random.uniform(splits[5], (HD,), jnp.float32, math.log(0.7), math.log(2.6))), 0.7, 2.6)
    attn_gate = jnp.clip(jax.random.uniform(splits[6], (1,), jnp.float32, 0.5, 2.0), 0.5, 2.0)
    image_ids_keys = jax.random.split(jax.random.fold_in(splits[7], 1), REQUESTS // RQ_DEV)
    image_ids_turns = jax.random.permutation(jax.random.fold_in(splits[7], 3), REQUESTS // RQ_DEV)
    image_ids = jax.vmap(lambda own, number: deal_out(jax.random.fold_in(splits[7], 2), own, number, RQ_DEV, NIMG, 2, CAP, 2))(image_ids_keys, image_ids_turns).reshape((REQUESTS, 2))
    image_slot = jax.random.permutation(splits[8], NIMG).astype(jnp.int32)
    return dict(text_rows=text_rows, q_weight=q_weight, features=features, kv_weight=kv_weight, q_gain=q_gain, k_gain=k_gain, attn_gate=attn_gate, image_ids=image_ids, image_slot=image_slot)


epsilon = 1e-05

def head_norm(values, gain_vector):
    return values * lax.rsqrt(lax.optimization_barrier(jnp.mean(values * values, axis=-1, keepdims=True)) + epsilon) * gain_vector

def reference(text_rows, q_weight, features, kv_weight, q_gain, k_gain, attn_gate, image_ids, image_slot):
    highest = lax.Precision.HIGHEST
    group_size = HEADS // KVH
    queries = jnp.dot(text_rows.astype(jnp.float32), q_weight.astype(jnp.float32), precision=highest)
    normed = head_norm(queries.reshape(ROWS, KVH, group_size, HD), q_gain) * HD ** (-0.5)
    normed = normed.astype(jnp.bfloat16).reshape(REQUESTS, TEXT, KVH, group_size, HD)
    kv_table = kv_weight.astype(jnp.float32)

    def project(vision_rows):
        summed = jnp.dot(vision_rows.astype(jnp.float32), kv_table, precision=highest).reshape(VT, KVH, 2 * HD)
        normed_keys = head_norm(summed[..., :HD], k_gain)
        return jnp.concatenate([normed_keys, summed[..., HD:]], axis=-1).astype(jnp.bfloat16)
    keyval = lax.map(project, features)
    owners = image_slot[image_ids].astype(jnp.int32)

    def answer(inputs):
        request_queries, pair_slots = inputs
        joined = jnp.concatenate([keyval[pair_slots[0]], keyval[pair_slots[1]]], axis=0).astype(jnp.float32)
        scores = jnp.einsum('thgd,nhd->thgn', request_queries.astype(jnp.float32), joined[..., :HD], precision=highest)
        exponent = jnp.exp(scores).astype(jnp.bfloat16).astype(jnp.float32)
        denominator = lax.optimization_barrier(jnp.sum(exponent, axis=-1))
        numerator = jnp.einsum('thgn,nhd->thgd', exponent, joined[..., HD:], precision=highest)
        return numerator / denominator[..., None]
    result = lax.map(answer, (normed, owners))
    return (jnp.tanh(attn_gate[0]) * result).astype(jnp.bfloat16).reshape(ROWS, HEADS * HD)
```

```python
import functools

import jax
import jax.numpy as jnp
from jax import lax
from jax.experimental import pallas as pl
from jax.experimental.pallas import tpu as pltpu
from jax.sharding import PartitionSpec as P

epsilon = 1e-05
MIB = 1024 * 1024
MESH = pl.DeviceIdType.MESH
HALVES = 2
SLOTS = 3
PIECE = 256


def head_norm(values, gain_vector):
    return (
        values
        * lax.rsqrt(jnp.mean(values * values, axis=-1, keepdims=True) + epsilon)
        * gain_vector
    )


def fused_kernel(
    sizes,
    ids_ref, slot_ref, gate_ref, text_ref, features_ref, q_gain_ref, k_gain_ref, q_weight_ref, kv_weight_ref,
    out_ref,
    vision, kv_table, outgoing, incoming, own, text_full, weights, queries, attended,
    vision_sem, table_sem, rs_send, rs_recv, text_send, text_recv, weight_sem, kv_send, kv_recv,
    *keyval,
):
    feat_count, dp_count, head_width, group, kv_local = sizes
    rows = text_ref.shape[0]
    requests = ids_ref.shape[0]
    text_words = rows // requests
    wide = 2 * head_width
    half_rows = vision.shape[1]
    chunks = kv_local * HALVES
    pieces = q_weight_ref.shape[1] // PIECE
    depth = text_ref.shape[1]
    positions = dp_count // 2
    me_feat, me_dp = lax.axis_index("feat"), lax.axis_index("dp")
    position, core = me_dp // 2, me_dp % 2
    sibling = me_dp + 1 - 2 * core

    def load_vision(half):
        return pltpu.make_async_copy(
            features_ref.at[pl.ds(half * half_rows, half_rows), :], vision.at[half], vision_sem.at[half]
        )

    def load_table(f, h):
        start = pl.multiple_of((f * kv_local + h) * wide, wide)
        return pltpu.make_async_copy(
            kv_weight_ref.at[:, pl.ds(start, wide)], kv_table.at[f, h], table_sem.at[f, h]
        )

    def load_weight(j):
        start = pl.multiple_of(j * PIECE, PIECE)
        return pltpu.make_async_copy(
            q_weight_ref.at[:, pl.ds(start, PIECE)], weights.at[j % SLOTS], weight_sem.at[j]
        )

    load_vision(0).start()
    for h in range(kv_local):
        for d in range(1, feat_count + 1):
            load_table((me_feat + d) % feat_count, h).start()
        if h == 0:
            for half in range(1, HALVES):
                load_vision(half).start()
    for j in range(min(SLOTS, pieces)):
        load_weight(j).start()

    barrier = pltpu.get_barrier_semaphore()
    for d in range(1, feat_count):
        pl.semaphore_signal(barrier, inc=1, device_id={"feat": (me_feat + d) % feat_count}, device_id_type=MESH)
    pl.semaphore_signal(barrier, inc=1, device_id={"dp": sibling}, device_id_type=MESH)

    @pl.when(position > 0)
    def _():
        pl.semaphore_signal(barrier, inc=1, device_id={"dp": me_dp - 2}, device_id_type=MESH)

    @pl.when(position < positions - 1)
    def _():
        pl.semaphore_signal(barrier, inc=1, device_id={"dp": me_dp + 2}, device_id_type=MESH)

    inside = (position > 0) & (position < positions - 1)

    @pl.when(inside)
    def _():
        pl.semaphore_wait(barrier, feat_count + 2)

    @pl.when(jnp.logical_not(inside))
    def _():
        pl.semaphore_wait(barrier, feat_count + min(1, positions - 1))

    text_full[me_feat] = text_ref[...]

    def text_copy(d):
        return pltpu.make_async_remote_copy(
            src_ref=text_ref, dst_ref=text_full.at[me_feat], send_sem=text_send.at[d - 1],
            recv_sem=text_recv.at[d - 1], device_id={"feat": (me_feat + d) % feat_count}, device_id_type=MESH,
        )

    def partial_copy(c, d):
        return pltpu.make_async_remote_copy(
            src_ref=outgoing.at[c, d - 1], dst_ref=incoming.at[c, d - 1], send_sem=rs_send.at[c, d - 1],
            recv_sem=rs_recv.at[c, d - 1], device_id={"feat": (me_feat + d) % feat_count}, device_id_type=MESH,
        )

    def share(c, origin, way, target):
        h, half = c // HALVES, c % HALVES
        block = keyval[h].at[origin, pl.ds(half * half_rows, half_rows), :]
        return pltpu.make_async_remote_copy(
            src_ref=block, dst_ref=block, send_sem=kv_send.at[way, c, origin],
            recv_sem=kv_recv.at[c, origin], device_id={"dp": target}, device_id_type=MESH,
        )

    for c in range(chunks):
        h, half = c // HALVES, c % HALVES
        if h == 0:
            load_vision(half).wait()

        def one_peer(d, carry, c=c, h=h, half=half):
            f = (me_feat + d) % feat_count
            if half == 0:
                load_table(f, h).wait()
            outgoing[c, d - 1] = jnp.dot(
                vision[half], kv_table[f, h], preferred_element_type=jnp.float32
            ).astype(jnp.bfloat16)
            partial_copy(c, d).start()
            return carry

        lax.fori_loop(1, feat_count, one_peer, 0)
        if half == 0:
            load_table(me_feat, h).wait()
        own[c] = jnp.dot(vision[half], kv_table[me_feat, h], preferred_element_type=jnp.float32)
        if c == max(0, chunks - 2):
            for d in range(1, feat_count):
                text_copy(d).start()

    def finish_own(c):
        h, half = c // HALVES, c % HALVES
        summed = own[c]
        for d in range(1, feat_count):
            partial_copy(c, d).wait_recv()
            summed = summed + incoming[c, d - 1].astype(jnp.float32)
        normed_keys = head_norm(summed[:, :head_width], k_gain_ref[...])
        block = jnp.concatenate([normed_keys, summed[:, head_width:]], axis=-1).astype(jnp.bfloat16)
        keyval[h][me_dp, half * half_rows : (half + 1) * half_rows, :] = block

        @pl.when(position > 0)
        def _():
            share(c, me_dp, 0, me_dp - 2).start()

        @pl.when(position < positions - 1)
        def _():
            share(c, me_dp, 1, me_dp + 2).start()

        share(c, me_dp, 2, sibling).start()

    def pass_on(c, distance):
        @pl.when(position >= distance)
        def _():
            origin = me_dp - 2 * distance
            share(c, origin, 1, sibling).wait_recv()

            @pl.when(position < positions - 1)
            def _():
                share(c, origin, 1, me_dp + 2).start()

            share(c, origin, 2, sibling).start()

        @pl.when(position + distance < positions)
        def _():
            origin = me_dp + 2 * distance
            share(c, origin, 0, sibling).wait_recv()

            @pl.when(position > 0)
            def _():
                share(c, origin, 0, me_dp - 2).start()

            share(c, origin, 2, sibling).start()

    def project(j, carry):
        load_weight(j).wait()
        total = jnp.zeros((rows, PIECE), jnp.float32)
        for f in range(feat_count):
            total += jnp.dot(
                text_full[f],
                weights[j % SLOTS, f * depth : (f + 1) * depth, :],
                preferred_element_type=jnp.float32,
            )
        for part in range(PIECE // head_width):
            normed = head_norm(total[:, part * head_width : (part + 1) * head_width], q_gain_ref[...])
            normed = (normed * head_width ** (-0.5)).astype(jnp.bfloat16)
            start = pl.multiple_of(j * PIECE + part * head_width, head_width)
            queries[:, pl.ds(start, head_width)] = normed.astype(jnp.float32)

        @pl.when(j + SLOTS < pieces)
        def _():
            load_weight(j + SLOTS).start()

        return carry

    gate = jnp.tanh(jnp.full((1, head_width), gate_ref[0], jnp.float32))
    ones = jnp.ones((HALVES * half_rows, head_width), jnp.bfloat16)

    def attend(h):
        for c in range(h * HALVES, (h + 1) * HALVES):
            for at in range(positions):
                share(c, at * 2 + 1 - core, 2, sibling).wait_recv()
        first = h * group * head_width

        def one_request(r, carry):
            span = pl.ds(pl.multiple_of(r * text_words, text_words), text_words)
            q = jnp.concatenate(
                [queries[span, first + g * head_width : first + (g + 1) * head_width] for g in range(group)], axis=0
            ).astype(jnp.bfloat16)
            total = jnp.zeros((group * text_words, wide), jnp.float32)
            for s in range(2):
                owner = slot_ref[ids_ref[r, s]]
                keys = keyval[h][owner, :, :head_width]
                values = keyval[h][owner, :, head_width:]
                scores = lax.dot_general(q, keys, (((1,), (1,)), ((), ())), preferred_element_type=jnp.float32)
                exponent = jnp.exp(scores).astype(jnp.bfloat16)
                total += jnp.dot(
                    exponent, jnp.concatenate([values, ones], axis=1), preferred_element_type=jnp.float32
                )
            result = gate * (total[:, :head_width] / total[:, head_width:])
            for g in range(group):
                attended[span, first + g * head_width : first + (g + 1) * head_width] = result[
                    g * text_words : (g + 1) * text_words
                ]
            return carry

        lax.fori_loop(0, requests, one_request, 0)

    ticks = chunks + positions - 1
    begun = 0
    for tick in range(ticks):
        for distance in range(positions - 1, 0, -1):
            if 0 <= tick - distance < chunks:
                pass_on(tick - distance, distance)
        if tick < chunks:
            finish_own(tick)
        if tick == chunks - 1:
            for d in range(1, feat_count):
                text_copy(d).wait_recv()
        if tick >= chunks - 1 and begun < pieces:
            until = pieces if tick >= min(chunks, ticks - 2) else pieces // 2
            lax.fori_loop(begun, until, project, 0)
            begun = until
        if tick == ticks - 2:
            for h in range(kv_local - 1):
                attend(h)
    attend(kv_local - 1)
    out_ref[...] = attended[...].astype(jnp.bfloat16)

    for c in range(chunks):
        for d in range(1, feat_count):
            partial_copy(c, d).wait_send()
        for at in range(positions):
            origin = at * 2 + core
            share(c, origin, 2, sibling).wait_send()

            @pl.when((position > 0) & (at >= position))
            def _():
                share(c, origin, 0, me_dp - 2).wait_send()

            @pl.when((position < positions - 1) & (at <= position))
            def _():
                share(c, origin, 1, me_dp + 2).wait_send()

    for d in range(1, feat_count):
        text_copy(d).wait_send()


def per_device(
    text_rows, q_weight, features, kv_weight, q_gain, k_gain, attn_gate, image_ids, image_slot
):
    rows, depth = text_rows.shape
    columns = q_weight.shape[1]
    head_width = q_gain.shape[0]
    wide = 2 * head_width
    feat_count, dp_count = lax.axis_size("feat"), lax.axis_size("dp")
    kv_local = kv_weight.shape[1] // wide // feat_count
    group = columns // (head_width * kv_local)
    tokens, width = features.shape[1:]
    half_rows = tokens // HALVES
    chunks = kv_local * HALVES
    smem = pl.BlockSpec(memory_space=pltpu.SMEM)
    vmem = pl.BlockSpec(memory_space=pltpu.VMEM)
    whole = pl.BlockSpec(memory_space=pl.ANY)
    dma = pltpu.SemaphoreType.DMA
    scratch = [
        pltpu.VMEM((HALVES, half_rows, width), jnp.bfloat16),
        pltpu.VMEM((feat_count, kv_local, width, wide), jnp.bfloat16),
        pltpu.VMEM((chunks, feat_count - 1, half_rows, wide), jnp.bfloat16),
        pltpu.VMEM((chunks, feat_count - 1, half_rows, wide), jnp.bfloat16),
        pltpu.VMEM((chunks, half_rows, wide), jnp.float32),
        pltpu.VMEM((feat_count, rows, depth), jnp.bfloat16),
        pltpu.VMEM((SLOTS, q_weight.shape[0], PIECE), jnp.bfloat16),
        pltpu.VMEM((rows, columns), jnp.float32),
        pltpu.VMEM((rows, columns), jnp.float32),
        dma((HALVES,)),
        dma((feat_count, kv_local)),
        dma((chunks, feat_count - 1)),
        dma((chunks, feat_count - 1)),
        dma((feat_count - 1,)),
        dma((feat_count - 1,)),
        dma((columns // PIECE,)),
        dma((3, chunks, dp_count)),
        dma((chunks, dp_count)),
    ] + [pltpu.VMEM((dp_count, tokens, wide), jnp.bfloat16) for _ in range(kv_local)]
    return pl.pallas_call(
        functools.partial(fused_kernel, (feat_count, dp_count, head_width, group, kv_local)),
        out_shape=jax.ShapeDtypeStruct((rows, columns), jnp.bfloat16),
        in_specs=[smem, smem, smem, vmem, whole, vmem, vmem, whole, whole],
        out_specs=vmem,
        scratch_shapes=scratch,
        compiler_params=pltpu.CompilerParams(
            collective_id=0, has_side_effects=True, vmem_limit_bytes=60 * MIB
        ),
        name="gated_cross_attention",
    )(
        image_ids, image_slot, attn_gate, text_rows, features[0],
        q_gain.reshape(1, -1), k_gain.reshape(1, -1), q_weight, kv_weight,
    )


def solution(mesh):
    in_specs = (
        P("dp", "feat"),
        P(None, "feat"),
        P("dp", None, "feat"),
        P("feat", None),
        P(),
        P(),
        P(),
        P("dp", None),
        P(),
    )
    out_specs = P("dp", "feat")
    return jax.shard_map(
        per_device, mesh=mesh, in_specs=in_specs, out_specs=out_specs, check_vma=False
    )
```

```python
import functools

import jax
import jax.numpy as jnp
from jax import lax
from jax.experimental import pallas as pl
from jax.experimental.pallas import tpu as pltpu
from jax.sharding import PartitionSpec as P

epsilon = 1e-05
MIB = 1024 * 1024
MESH = pl.DeviceIdType.MESH
HALVES = 4
SLOTS = 4
PIECE = 256


def head_norm(values, gain_vector):
    return (
        values
        * lax.rsqrt(jnp.mean(values * values, axis=-1, keepdims=True) + epsilon)
        * gain_vector
    )


def fused_kernel(
    sizes,
    ids_ref, slot_ref, gate_ref, text_ref, features_ref, q_gain_ref, k_gain_ref, q_weight_ref, kv_weight_ref,
    out_ref,
    vision, kv_table, outgoing, incoming, own, text_full, weights, queries, grouped, sums, attended,
    vision_sem, table_sem, rs_send, rs_recv, text_send, text_recv, weight_sem, kv_send, kv_recv,
    *keyval,
):
    feat_count, dp_count, head_width, group, kv_local = sizes
    rows = text_ref.shape[0]
    requests = ids_ref.shape[0]
    text_words = rows // requests
    wide = 2 * head_width
    half_rows = vision.shape[1]
    chunks = kv_local * HALVES
    pieces = q_weight_ref.shape[1] // PIECE
    depth = text_ref.shape[1]
    positions = dp_count // 2
    me_feat, me_dp = lax.axis_index("feat"), lax.axis_index("dp")
    position, core = me_dp // 2, me_dp % 2
    sibling = me_dp + 1 - 2 * core

    def load_vision(half):
        return pltpu.make_async_copy(
            features_ref.at[pl.ds(half * half_rows, half_rows), :], vision.at[half], vision_sem.at[half]
        )

    def load_table(f, h):
        start = pl.multiple_of((f * kv_local + h) * wide, wide)
        return pltpu.make_async_copy(
            kv_weight_ref.at[:, pl.ds(start, wide)], kv_table.at[f, h], table_sem.at[f, h]
        )

    def load_weight(j):
        start = pl.multiple_of(j * PIECE, PIECE)
        return pltpu.make_async_copy(
            q_weight_ref.at[:, pl.ds(start, PIECE)], weights.at[j % SLOTS], weight_sem.at[j]
        )

    load_vision(0).start()
    for h in range(kv_local):
        for d in range(1, feat_count + 1):
            load_table((me_feat + d) % feat_count, h).start()
        if h == 0:
            for half in range(1, HALVES):
                load_vision(half).start()
    for j in range(min(SLOTS, pieces)):
        load_weight(j).start()

    barrier = pltpu.get_barrier_semaphore()
    for d in range(1, feat_count):
        pl.semaphore_signal(barrier, inc=1, device_id={"feat": (me_feat + d) % feat_count}, device_id_type=MESH)
    pl.semaphore_signal(barrier, inc=1, device_id={"dp": sibling}, device_id_type=MESH)

    @pl.when(position > 0)
    def _():
        pl.semaphore_signal(barrier, inc=1, device_id={"dp": me_dp - 2}, device_id_type=MESH)

    @pl.when(position < positions - 1)
    def _():
        pl.semaphore_signal(barrier, inc=1, device_id={"dp": me_dp + 2}, device_id_type=MESH)

    inside = (position > 0) & (position < positions - 1)

    @pl.when(inside)
    def _():
        pl.semaphore_wait(barrier, feat_count + 2)

    @pl.when(jnp.logical_not(inside))
    def _():
        pl.semaphore_wait(barrier, feat_count + min(1, positions - 1))

    text_full[me_feat] = text_ref[...]

    def text_copy(d):
        return pltpu.make_async_remote_copy(
            src_ref=text_ref, dst_ref=text_full.at[me_feat], send_sem=text_send.at[d - 1],
            recv_sem=text_recv.at[d - 1], device_id={"feat": (me_feat + d) % feat_count}, device_id_type=MESH,
        )

    def partial_copy(c, d):
        return pltpu.make_async_remote_copy(
            src_ref=outgoing.at[c, d - 1], dst_ref=incoming.at[c, d - 1], send_sem=rs_send.at[c, d - 1],
            recv_sem=rs_recv.at[c, d - 1], device_id={"feat": (me_feat + d) % feat_count}, device_id_type=MESH,
        )

    def share(c, origin, way, target):
        block = keyval[c].at[origin]
        return pltpu.make_async_remote_copy(
            src_ref=block, dst_ref=block, send_sem=kv_send.at[way, c, origin],
            recv_sem=kv_recv.at[c, origin], device_id={"dp": target}, device_id_type=MESH,
        )

    for c in range(chunks):
        h, half = c // HALVES, c % HALVES
        if h == 0:
            load_vision(half).wait()

        def one_peer(d, carry, c=c, h=h, half=half):
            f = (me_feat + d) % feat_count
            if half == 0:
                load_table(f, h).wait()
            outgoing[c, d - 1] = jnp.dot(
                vision[half], kv_table[f, h], preferred_element_type=jnp.float32
            ).astype(jnp.bfloat16)
            partial_copy(c, d).start()
            return carry

        lax.fori_loop(1, feat_count, one_peer, 0)
        if half == 0:
            load_table(me_feat, h).wait()
        own[c] = jnp.dot(vision[half], kv_table[me_feat, h], preferred_element_type=jnp.float32)
        for d in range(1, feat_count):
            if c == min(chunks - 1, chunks // 4 + d - 1):
                text_copy(d).start()

    def finish_own(c):
        summed = own[c]
        for d in range(1, feat_count):
            partial_copy(c, d).wait_recv()
            summed = summed + incoming[c, d - 1].astype(jnp.float32)
        normed_keys = head_norm(summed[:, :head_width], k_gain_ref[...])
        turned = jnp.concatenate(
            [normed_keys[at : at + head_width].T for at in range(0, half_rows, head_width)], axis=0
        )
        keyval[c][me_dp] = jnp.concatenate([turned, summed[:, head_width:]], axis=-1).astype(jnp.bfloat16)

        @pl.when(position > 0)
        def _():
            share(c, me_dp, 0, me_dp - 2).start()

        @pl.when(position < positions - 1)
        def _():
            share(c, me_dp, 1, me_dp + 2).start()

        share(c, me_dp, 2, sibling).start()

    def pass_on(c, distance):
        @pl.when(position >= distance)
        def _():
            origin = me_dp - 2 * distance
            share(c, origin, 1, sibling).wait_recv()

            @pl.when(position < positions - 1)
            def _():
                share(c, origin, 1, me_dp + 2).start()

            share(c, origin, 2, sibling).start()

        @pl.when(position + distance < positions)
        def _():
            origin = me_dp + 2 * distance
            share(c, origin, 0, sibling).wait_recv()

            @pl.when(position > 0)
            def _():
                share(c, origin, 0, me_dp - 2).start()

            share(c, origin, 2, sibling).start()

    def project(j, carry):
        load_weight(j).wait()
        total = jnp.zeros((rows, PIECE), jnp.float32)
        for f in range(feat_count):
            total += jnp.dot(
                text_full[f],
                weights[j % SLOTS, f * depth : (f + 1) * depth, :],
                preferred_element_type=jnp.float32,
            )
        for part in range(PIECE // head_width):
            normed = head_norm(total[:, part * head_width : (part + 1) * head_width], q_gain_ref[...])
            normed = (normed * head_width ** (-0.5)).astype(jnp.bfloat16)
            start = pl.multiple_of(j * PIECE + part * head_width, head_width)
            queries[:, pl.ds(start, head_width)] = normed.astype(jnp.float32)

        @pl.when(j + SLOTS < pieces)
        def _():
            load_weight(j + SLOTS).start()

        return carry

    def regroup(r, carry):
        span = pl.ds(pl.multiple_of(r * text_words, text_words), text_words)
        for h in range(kv_local):
            first = h * group * head_width
            grouped[h, r] = jnp.concatenate(
                [queries[span, first + g * head_width : first + (g + 1) * head_width] for g in range(group)], axis=0
            ).astype(jnp.bfloat16)
        return carry

    gate = jnp.tanh(jnp.full((1, head_width), gate_ref[0], jnp.float32))
    ones = jnp.ones((2 * half_rows, head_width), jnp.bfloat16)

    def attend(c):
        h, half = c // HALVES, c % HALVES
        for at in range(positions):
            share(c, at * 2 + 1 - core, 2, sibling).wait_recv()
        first = h * group * head_width

        def one_request(r, carry):
            owners = [slot_ref[ids_ref[r, s]] for s in range(2)]
            keys = jnp.concatenate(
                [
                    keyval[c][owner, at : at + head_width, :head_width]
                    for owner in owners
                    for at in range(0, half_rows, head_width)
                ],
                axis=1,
            )
            values = jnp.concatenate([keyval[c][owner, :, head_width:] for owner in owners], axis=0)
            scores = jnp.dot(grouped[h, r], keys, preferred_element_type=jnp.float32)
            exponent = jnp.exp(scores).astype(jnp.bfloat16)
            total = jnp.dot(
                exponent, jnp.concatenate([values, ones], axis=1), preferred_element_type=jnp.float32
            )
            if half > 0:
                total += sums[r]
            if half < HALVES - 1:
                sums[r] = total
                return carry
            span = pl.ds(pl.multiple_of(r * text_words, text_words), text_words)
            result = gate * (total[:, :head_width] / total[:, head_width:])
            for g in range(group):
                attended[span, first + g * head_width : first + (g + 1) * head_width] = result[
                    g * text_words : (g + 1) * text_words
                ]
            return carry

        lax.fori_loop(0, requests, one_request, 0, unroll=2)

    ticks = chunks + positions - 1
    begun = ready = 0
    project_at = max(1, chunks - 3)
    for tick in range(ticks):
        for distance in range(positions - 1, 0, -1):
            if 0 <= tick - distance < chunks:
                pass_on(tick - distance, distance)
        if tick < chunks:
            finish_own(tick)
        if tick == project_at:
            for d in range(1, feat_count):
                text_copy(d).wait_recv()
        if tick >= project_at and begun < pieces:
            until = min(pieces, begun + (pieces + 1) // 2)
            lax.fori_loop(begun, until, project, 0)
            begun = until
            if begun == pieces:
                lax.fori_loop(0, requests, regroup, 0)
        elif begun == pieces:
            for _ in range(2):
                if ready <= tick - positions and ready < chunks:
                    attend(ready)
                    ready += 1
    for c in range(ready, chunks):
        attend(c)
    out_ref[...] = attended[...].astype(jnp.bfloat16)

    for c in range(chunks):
        for d in range(1, feat_count):
            partial_copy(c, d).wait_send()
        for at in range(positions):
            origin = at * 2 + core
            share(c, origin, 2, sibling).wait_send()

            @pl.when((position > 0) & (at >= position))
            def _():
                share(c, origin, 0, me_dp - 2).wait_send()

            @pl.when((position < positions - 1) & (at <= position))
            def _():
                share(c, origin, 1, me_dp + 2).wait_send()

    for d in range(1, feat_count):
        text_copy(d).wait_send()


def per_device(
    text_rows, q_weight, features, kv_weight, q_gain, k_gain, attn_gate, image_ids, image_slot
):
    rows, depth = text_rows.shape
    columns = q_weight.shape[1]
    head_width = q_gain.shape[0]
    wide = 2 * head_width
    feat_count, dp_count = lax.axis_size("feat"), lax.axis_size("dp")
    kv_local = kv_weight.shape[1] // wide // feat_count
    group = columns // (head_width * kv_local)
    tokens, width = features.shape[1:]
    half_rows = tokens // HALVES
    requests = image_ids.shape[0]
    chunks = kv_local * HALVES
    smem = pl.BlockSpec(memory_space=pltpu.SMEM)
    vmem = pl.BlockSpec(memory_space=pltpu.VMEM)
    whole = pl.BlockSpec(memory_space=pl.ANY)
    dma = pltpu.SemaphoreType.DMA
    scratch = [
        pltpu.VMEM((HALVES, half_rows, width), jnp.bfloat16),
        pltpu.VMEM((feat_count, kv_local, width, wide), jnp.bfloat16),
        pltpu.VMEM((chunks, feat_count - 1, half_rows, wide), jnp.bfloat16),
        pltpu.VMEM((chunks, feat_count - 1, half_rows, wide), jnp.bfloat16),
        pltpu.VMEM((chunks, half_rows, wide), jnp.float32),
        pltpu.VMEM((feat_count, rows, depth), jnp.bfloat16),
        pltpu.VMEM((SLOTS, q_weight.shape[0], PIECE), jnp.bfloat16),
        pltpu.VMEM((rows, columns), jnp.float32),
        pltpu.VMEM((kv_local, requests, group * rows // requests, head_width), jnp.bfloat16),
        pltpu.VMEM((requests, group * rows // requests, wide), jnp.float32),
        pltpu.VMEM((rows, columns), jnp.float32),
        dma((HALVES,)),
        dma((feat_count, kv_local)),
        dma((chunks, feat_count - 1)),
        dma((chunks, feat_count - 1)),
        dma((feat_count - 1,)),
        dma((feat_count - 1,)),
        dma((columns // PIECE,)),
        dma((3, chunks, dp_count)),
        dma((chunks, dp_count)),
    ] + [pltpu.VMEM((dp_count, half_rows, wide), jnp.bfloat16) for _ in range(chunks)]
    return pl.pallas_call(
        functools.partial(fused_kernel, (feat_count, dp_count, head_width, group, kv_local)),
        out_shape=jax.ShapeDtypeStruct((rows, columns), jnp.bfloat16),
        in_specs=[smem, smem, smem, vmem, whole, vmem, vmem, whole, whole],
        out_specs=vmem,
        scratch_shapes=scratch,
        compiler_params=pltpu.CompilerParams(
            collective_id=0, has_side_effects=True, vmem_limit_bytes=60 * MIB
        ),
        name="gated_cross_attention",
    )(
        image_ids, image_slot, attn_gate, text_rows, features[0],
        q_gain.reshape(1, -1), k_gain.reshape(1, -1), q_weight, kv_weight,
    )


def solution(mesh):
    in_specs = (
        P("dp", "feat"),
        P(None, "feat"),
        P("dp", None, "feat"),
        P("feat", None),
        P(),
        P(),
        P(),
        P("dp", None),
        P(),
    )
    out_specs = P("dp", "feat")
    return jax.shard_map(
        per_device, mesh=mesh, in_specs=in_specs, out_specs=out_specs, check_vma=False
    )
```

```python
import functools

import jax
import jax.numpy as jnp
from jax import lax
from jax.experimental import pallas as pl
from jax.experimental.pallas import tpu as pltpu
from jax.sharding import PartitionSpec as P

epsilon = 1e-05
MIB = 1024 * 1024
MESH = pl.DeviceIdType.MESH
HALVES = 4
SLOTS = 8
PIECE = 512
LEAD = 4


def head_norm(values, gain_vector):
    return (
        values
        * lax.rsqrt(jnp.mean(values * values, axis=-1, keepdims=True) + epsilon)
        * gain_vector
    )


def fused_kernel(
    sizes,
    ids_ref, slot_ref, gate_ref, text_ref, features_ref, q_gain_ref, k_gain_ref, q_weight_ref, kv_weight_ref,
    out_ref,
    vision, kv_table, outgoing, incoming, own, text_full, weights, queries, grouped, sums, attended,
    vision_sem, table_sem, rs_send, rs_recv, text_send, text_recv, weight_sem, kv_send, kv_recv,
    *keyval,
):
    feat_count, dp_count, head_width, group, kv_local = sizes
    rows = text_ref.shape[0]
    requests = ids_ref.shape[0]
    text_words = rows // requests
    wide = 2 * head_width
    half_rows = vision.shape[1]
    chunks = kv_local * HALVES
    across = q_weight_ref.shape[1] // PIECE
    pieces = feat_count * across
    depth = text_ref.shape[1]
    positions = dp_count // 2
    me_feat, me_dp = lax.axis_index("feat"), lax.axis_index("dp")
    position, core = me_dp // 2, me_dp % 2
    sibling = me_dp + 1 - 2 * core

    def load_vision(half):
        return pltpu.make_async_copy(
            features_ref.at[pl.ds(half * half_rows, half_rows), :], vision.at[half], vision_sem.at[half]
        )

    def load_table(f, h):
        start = pl.multiple_of((f * kv_local + h) * wide, wide)
        return pltpu.make_async_copy(
            kv_weight_ref.at[:, pl.ds(start, wide)], kv_table.at[f, h], table_sem.at[f, h]
        )

    def load_weight(j):
        source = (me_feat - j // across + feat_count) % feat_count
        down = pl.multiple_of(source * depth, depth)
        start = pl.multiple_of(j % across * PIECE, PIECE)
        return pltpu.make_async_copy(
            q_weight_ref.at[pl.ds(down, depth), pl.ds(start, PIECE)], weights.at[j % SLOTS], weight_sem.at[j]
        )

    load_vision(0).start()
    for h in range(kv_local):
        for d in range(1, feat_count + 1):
            load_table((me_feat + d) % feat_count, h).start()
        if h == 0:
            for half in range(1, HALVES):
                load_vision(half).start()
    for j in range(min(SLOTS, pieces)):
        load_weight(j).start()

    barrier = pltpu.get_barrier_semaphore()
    for d in range(1, feat_count):
        pl.semaphore_signal(barrier, inc=1, device_id={"feat": (me_feat + d) % feat_count}, device_id_type=MESH)
    pl.semaphore_signal(barrier, inc=1, device_id={"dp": sibling}, device_id_type=MESH)

    @pl.when(position > 0)
    def _():
        pl.semaphore_signal(barrier, inc=1, device_id={"dp": me_dp - 2}, device_id_type=MESH)

    @pl.when(position < positions - 1)
    def _():
        pl.semaphore_signal(barrier, inc=1, device_id={"dp": me_dp + 2}, device_id_type=MESH)

    inside = (position > 0) & (position < positions - 1)

    @pl.when(inside)
    def _():
        pl.semaphore_wait(barrier, feat_count + 2)

    @pl.when(jnp.logical_not(inside))
    def _():
        pl.semaphore_wait(barrier, feat_count + min(1, positions - 1))

    text_full[me_feat] = text_ref[...]

    def text_copy(d):
        return pltpu.make_async_remote_copy(
            src_ref=text_ref, dst_ref=text_full.at[me_feat], send_sem=text_send.at[d - 1],
            recv_sem=text_recv.at[d - 1], device_id={"feat": (me_feat + d) % feat_count}, device_id_type=MESH,
        )

    def partial_copy(c, d):
        return pltpu.make_async_remote_copy(
            src_ref=outgoing.at[c, d - 1], dst_ref=incoming.at[c, d - 1], send_sem=rs_send.at[c, d - 1],
            recv_sem=rs_recv.at[c, d - 1], device_id={"feat": (me_feat + d) % feat_count}, device_id_type=MESH,
        )

    def share(c, origin, way, target):
        block = keyval[c].at[origin]
        return pltpu.make_async_remote_copy(
            src_ref=block, dst_ref=block, send_sem=kv_send.at[way, c, origin],
            recv_sem=kv_recv.at[c, origin], device_id={"dp": target}, device_id_type=MESH,
        )

    def project_piece(c):
        h, half = c // HALVES, c % HALVES
        if h == 0:
            load_vision(half).wait()

        def one_peer(d, carry):
            f = (me_feat + d) % feat_count
            if half == 0:
                load_table(f, h).wait()
            outgoing[c, d - 1] = jnp.dot(
                vision[half], kv_table[f, h], preferred_element_type=jnp.float32
            ).astype(jnp.bfloat16)
            partial_copy(c, d).start()
            return carry

        lax.fori_loop(1, feat_count, one_peer, 0)
        if half == 0:
            load_table(me_feat, h).wait()
        own[c] = jnp.dot(vision[half], kv_table[me_feat, h], preferred_element_type=jnp.float32)
        for d in range(1, feat_count):
            if c == min(chunks - 1, chunks // 2 - 2 + d):
                text_copy(d).start()

    def finish_own(c):
        summed = own[c]
        for d in range(1, feat_count):
            partial_copy(c, d).wait_recv()
            summed = summed + incoming[c, d - 1].astype(jnp.float32)
        normed_keys = head_norm(summed[:, :head_width], k_gain_ref[...])
        turned = jnp.concatenate(
            [normed_keys[at : at + head_width].T for at in range(0, half_rows, head_width)], axis=0
        )
        keyval[c][me_dp] = jnp.concatenate([turned, summed[:, head_width:]], axis=-1).astype(jnp.bfloat16)

        @pl.when(position > 0)
        def _():
            share(c, me_dp, 0, me_dp - 2).start()

        @pl.when(position < positions - 1)
        def _():
            share(c, me_dp, 1, me_dp + 2).start()

        share(c, me_dp, 2, sibling).start()

    def pass_on(c, distance):
        @pl.when(position >= distance)
        def _():
            origin = me_dp - 2 * distance
            share(c, origin, 1, sibling).wait_recv()

            @pl.when(position < positions - 1)
            def _():
                share(c, origin, 1, me_dp + 2).start()

            share(c, origin, 2, sibling).start()

        @pl.when(position + distance < positions)
        def _():
            origin = me_dp + 2 * distance
            share(c, origin, 0, sibling).wait_recv()

            @pl.when(position > 0)
            def _():
                share(c, origin, 0, me_dp - 2).start()

            share(c, origin, 2, sibling).start()

    def project(j, carry):
        load_weight(j).wait()
        source = (me_feat - j // across + feat_count) % feat_count
        columns = pl.ds(pl.multiple_of(j % across * PIECE, PIECE), PIECE)
        queries[:, columns] += jnp.dot(
            text_full[source], weights[j % SLOTS], preferred_element_type=jnp.float32
        )

        @pl.when(j + SLOTS < pieces)
        def _():
            load_weight(j + SLOTS).start()

        return carry

    def norm_queries():
        for at in range(0, queries.shape[1], head_width):
            normed = head_norm(queries[:, at : at + head_width], q_gain_ref[...])
            queries[:, at : at + head_width] = normed * head_width ** (-0.5)

    def regroup(r, carry):
        span = pl.ds(pl.multiple_of(r * text_words, text_words), text_words)
        for h in range(kv_local):
            first = h * group * head_width
            grouped[h, r] = jnp.concatenate(
                [queries[span, first + g * head_width : first + (g + 1) * head_width] for g in range(group)], axis=0
            ).astype(jnp.bfloat16)
        return carry

    gate = jnp.tanh(jnp.full((1, head_width), gate_ref[0], jnp.float32))
    ones = jnp.ones((2 * half_rows, head_width), jnp.bfloat16)

    def attend(c):
        h, half = c // HALVES, c % HALVES
        for at in range(positions):
            share(c, at * 2 + 1 - core, 2, sibling).wait_recv()
        first = h * group * head_width

        def one_request(r, carry):
            owners = [slot_ref[ids_ref[r, s]] for s in range(2)]
            keys = jnp.concatenate(
                [
                    keyval[c][owner, at : at + head_width, :head_width]
                    for owner in owners
                    for at in range(0, half_rows, head_width)
                ],
                axis=1,
            )
            values = jnp.concatenate([keyval[c][owner, :, head_width:] for owner in owners], axis=0)
            scores = jnp.dot(grouped[h, r], keys, preferred_element_type=jnp.float32)
            exponent = jnp.exp(scores).astype(jnp.bfloat16)
            total = jnp.dot(
                exponent, jnp.concatenate([values, ones], axis=1), preferred_element_type=jnp.float32
            )
            if half > 0:
                total += sums[r]
            if half < HALVES - 1:
                sums[r] = total
                return carry
            span = pl.ds(pl.multiple_of(r * text_words, text_words), text_words)
            result = gate * (total[:, :head_width] / total[:, head_width:])
            for g in range(group):
                attended[span, first + g * head_width : first + (g + 1) * head_width] = result[
                    g * text_words : (g + 1) * text_words
                ]
            return carry

        lax.fori_loop(0, requests, one_request, 0, unroll=2)

    ticks = chunks + positions - 1
    ready = 0
    queries[...] = jnp.zeros_like(queries)
    project_piece(0)
    for step in range(1, ticks + LEAD):
        if step < chunks:
            project_piece(step)
        tick = step - LEAD
        if tick < 0:
            continue
        for distance in range(positions - 1, 0, -1):
            if 0 <= tick - distance < chunks:
                pass_on(tick - distance, distance)
        if tick < chunks:
            finish_own(tick)
        due = [d for d in range(feat_count) if min(chunks // 2 - 1 + d if d else 0, ticks - 2) == tick]
        for d in due:
            if d > 0:
                text_copy(d).wait_recv()
            lax.fori_loop(d * across, (d + 1) * across, project, 0)
        if feat_count - 1 in due:
            norm_queries()
            lax.fori_loop(0, requests, regroup, 0)
        elif tick > min(chunks // 2 + feat_count - 2, ticks - 2):
            for _ in range(2):
                if ready <= tick - positions and ready < chunks:
                    attend(ready)
                    ready += 1
    for c in range(ready, chunks):
        attend(c)
    out_ref[...] = attended[...].astype(jnp.bfloat16)

    for c in range(chunks):
        for d in range(1, feat_count):
            partial_copy(c, d).wait_send()
        for at in range(positions):
            origin = at * 2 + core
            share(c, origin, 2, sibling).wait_send()

            @pl.when((position > 0) & (at >= position))
            def _():
                share(c, origin, 0, me_dp - 2).wait_send()

            @pl.when((position < positions - 1) & (at <= position))
            def _():
                share(c, origin, 1, me_dp + 2).wait_send()

    for d in range(1, feat_count):
        text_copy(d).wait_send()


def per_device(
    text_rows, q_weight, features, kv_weight, q_gain, k_gain, attn_gate, image_ids, image_slot
):
    rows, depth = text_rows.shape
    columns = q_weight.shape[1]
    head_width = q_gain.shape[0]
    wide = 2 * head_width
    feat_count, dp_count = lax.axis_size("feat"), lax.axis_size("dp")
    kv_local = kv_weight.shape[1] // wide // feat_count
    group = columns // (head_width * kv_local)
    tokens, width = features.shape[1:]
    half_rows = tokens // HALVES
    requests = image_ids.shape[0]
    chunks = kv_local * HALVES
    smem = pl.BlockSpec(memory_space=pltpu.SMEM)
    vmem = pl.BlockSpec(memory_space=pltpu.VMEM)
    whole = pl.BlockSpec(memory_space=pl.ANY)
    dma = pltpu.SemaphoreType.DMA
    scratch = [
        pltpu.VMEM((HALVES, half_rows, width), jnp.bfloat16),
        pltpu.VMEM((feat_count, kv_local, width, wide), jnp.bfloat16),
        pltpu.VMEM((chunks, feat_count - 1, half_rows, wide), jnp.bfloat16),
        pltpu.VMEM((chunks, feat_count - 1, half_rows, wide), jnp.bfloat16),
        pltpu.VMEM((chunks, half_rows, wide), jnp.float32),
        pltpu.VMEM((feat_count, rows, depth), jnp.bfloat16),
        pltpu.VMEM((SLOTS, depth, PIECE), jnp.bfloat16),
        pltpu.VMEM((rows, columns), jnp.float32),
        pltpu.VMEM((kv_local, requests, group * rows // requests, head_width), jnp.bfloat16),
        pltpu.VMEM((requests, group * rows // requests, wide), jnp.float32),
        pltpu.VMEM((rows, columns), jnp.float32),
        dma((HALVES,)),
        dma((feat_count, kv_local)),
        dma((chunks, feat_count - 1)),
        dma((chunks, feat_count - 1)),
        dma((feat_count - 1,)),
        dma((feat_count - 1,)),
        dma((feat_count * columns // PIECE,)),
        dma((3, chunks, dp_count)),
        dma((chunks, dp_count)),
    ] + [pltpu.VMEM((dp_count, half_rows, wide), jnp.bfloat16) for _ in range(chunks)]
    return pl.pallas_call(
        functools.partial(fused_kernel, (feat_count, dp_count, head_width, group, kv_local)),
        out_shape=jax.ShapeDtypeStruct((rows, columns), jnp.bfloat16),
        in_specs=[smem, smem, smem, vmem, whole, vmem, vmem, whole, whole],
        out_specs=vmem,
        scratch_shapes=scratch,
        compiler_params=pltpu.CompilerParams(
            collective_id=0, has_side_effects=True, vmem_limit_bytes=60 * MIB
        ),
        name="gated_cross_attention",
    )(
        image_ids, image_slot, attn_gate, text_rows, features[0],
        q_gain.reshape(1, -1), k_gain.reshape(1, -1), q_weight, kv_weight,
    )


def solution(mesh):
    in_specs = (
        P("dp", "feat"),
        P(None, "feat"),
        P("dp", None, "feat"),
        P("feat", None),
        P(),
        P(),
        P(),
        P("dp", None),
        P(),
    )
    out_specs = P("dp", "feat")
    return jax.shard_map(
        per_device, mesh=mesh, in_specs=in_specs, out_specs=out_specs, check_vma=False
    )
```
